32 devices in a mesh: ctx: 32 (over z, y, x, core), hid: 1.
Axes of the slice: x: 2, y: 2, z: 4, core: 2. Of those that a mesh axis runs over, the one named last changes fastest.
Arguments:
- queries: bfloat16 [8192, 4096], P('ctx', 'hid'), may hold values from -8 to 8
- keys: bfloat16 [8192, 1024], P('ctx', 'hid'), may hold values from -5 to 5
- values: bfloat16 [8192, 1024], P('ctx', 'hid'), may hold values from -6 to 6
- residual: bfloat16 [8192, 4096], P('ctx', 'hid'), may hold values from -6 to 6
- out_weight: bfloat16 [4096, 4096], P('hid'), may hold values from -0.09375 to 0.09375
Outputs:
- layer_out: bfloat16 [8192, 4096], P('ctx', 'hid')
The draws below stay inside these ranges and needn't reach their ends.
All inputs are finite; a program needn't handle non-finite values.
Results may differ from the reference program's by a relative error of at most 0.0044.
Values may be sent and summed in bfloat16 or wider, within the bound.
A program may use at most 128 MiB of HBM per device.

```python
import math
import jax
import jax.numpy as jnp
from jax import lax

D = 4096
QUERY_HEADS = 32
KEY_VALUE_HEADS = 8
HEAD_SIZE = 128
TOK_DEV = 256
SEQUENCE_LENGTH = 8192
N_CTX = 32


def joint_draw(key):
    base = jax.random.fold_in(key, 7)
    query_key, key_sampler = jax.random.split(base)
    queries = jnp.clip(jax.random.normal(query_key, (SEQUENCE_LENGTH, QUERY_HEADS * HEAD_SIZE), jnp.float32), -5.0, 5.0)
    keys = jnp.clip(jax.random.normal(key_sampler, (SEQUENCE_LENGTH, KEY_VALUE_HEADS * HEAD_SIZE), jnp.float32), -5.0, 5.0)
    return (queries, keys)


def draw_queries(key, part):
    return joint_draw(key)[0].astype(jnp.bfloat16)


def draw_keys(key, part):
    return joint_draw(key)[1].astype(jnp.bfloat16)


def level_of(stream_key, extent, shards, low, high):
    factor_of = 1.0
    for axis_at, blocks in shards:
        draws = jax.random.uniform(jax.random.fold_in(jax.random.fold_in(stream_key, 6), axis_at), (blocks,), jnp.float32, low / len(shards), high / len(shards))
        factor_of = factor_of * jnp.repeat(jnp.exp(draws), extent[axis_at] // blocks).reshape((-1,) + (1,) * (len(extent) - 1 - axis_at))
    return factor_of


def gaussian(stream_key, shape, deviation, most, cuts=(), kind=jnp.bfloat16):
    values = deviation * jax.random.normal(stream_key, shape, jnp.float32)
    if cuts:
        values = values * level_of(stream_key, shape, cuts, -0.22, 0.18)
    return jnp.clip(values, -most, most).astype(kind)


def setup_inputs(seed: int = 0) -> dict:
    streams_of = jax.random.split(jax.random.key(seed), 6)
    return {
        "queries": draw_queries(jax.random.fold_in(streams_of[5], 71), 0),
        "keys": draw_keys(jax.random.fold_in(streams_of[5], 71), 0),
        "values": gaussian(streams_of[2], (SEQUENCE_LENGTH, KEY_VALUE_HEADS * HEAD_SIZE), 1.0, 6.0, ((0, 32),)),
        "residual": gaussian(streams_of[3], (SEQUENCE_LENGTH, D), 1.0, 6.0, ((0, 32),)),
        "out_weight": gaussian(streams_of[4], (QUERY_HEADS * HEAD_SIZE, D), (QUERY_HEADS * HEAD_SIZE) ** -0.5, 0.09375),
    }


def block_mask(local_rows, position):
    row_ids = lax.broadcasted_iota(jnp.int32, (local_rows, 5 * local_rows), 0)
    col_ids = lax.broadcasted_iota(jnp.int32, (local_rows, 5 * local_rows), 1)
    block_ids = col_ids // local_rows
    offset = col_ids - block_ids * local_rows
    distance = jnp.where(block_ids == 0, 0, jnp.left_shift(jnp.int32(1), jnp.maximum(block_ids - 1, 0)))
    return jnp.where(block_ids == 0, offset <= row_ids, position >= distance)

def attend(query_matrix, gathered_rows, position):
    local_rows = query_matrix.shape[0]
    queries_per_group = QUERY_HEADS // KEY_VALUE_HEADS
    reshaped_output = query_matrix.astype(jnp.float32).reshape(local_rows, KEY_VALUE_HEADS, queries_per_group, HEAD_SIZE)
    key_matrix = gathered_rows[0].astype(jnp.float32).reshape(-1, KEY_VALUE_HEADS, HEAD_SIZE)
    value_matrix = gathered_rows[1].astype(jnp.float32).reshape(-1, KEY_VALUE_HEADS, HEAD_SIZE)
    scores = jnp.einsum('qkgd,skd->kgqs', reshaped_output, key_matrix) / math.sqrt(HEAD_SIZE)
    scores = jnp.where(block_mask(local_rows, position), scores, -1e+30)
    row_peak = lax.optimization_barrier(jnp.max(scores, axis=-1, keepdims=True))
    raised = jnp.exp(scores - row_peak)
    weights = (raised / lax.optimization_barrier(jnp.sum(raised, axis=-1, keepdims=True))).astype(jnp.bfloat16)
    mixed = jnp.einsum('kgqs,skd->qkgd', weights.astype(jnp.float32), value_matrix)
    return mixed.reshape(local_rows, QUERY_HEADS * HEAD_SIZE).astype(jnp.bfloat16)

def reference(queries, keys, values, residual, out_weight):
    stacked = jnp.stack([keys, values])
    weight_wide = out_weight.astype(jnp.float32)

    def one_block(position):
        parts = []
        for distance in (0, 1, 2, 4, 8):
            source_block = (jnp.maximum(position - distance, 0) * TOK_DEV).astype(jnp.int32)
            parts.append(lax.dynamic_slice_in_dim(stacked, source_block, TOK_DEV, 1))
        gathered_rows = jnp.concatenate(parts, axis=1)
        first_row = (position * TOK_DEV).astype(jnp.int32)
        query_matrix = lax.dynamic_slice_in_dim(queries, first_row, TOK_DEV, 0)
        attended = attend(query_matrix, gathered_rows, position)
        projected = jnp.dot(attended.astype(jnp.float32), weight_wide)
        stream = lax.dynamic_slice_in_dim(residual, first_row, TOK_DEV, 0).astype(jnp.float32)
        return (stream + projected).astype(jnp.bfloat16)
    blocks_out = lax.map(one_block, jnp.arange(N_CTX, dtype=jnp.int32))
    return blocks_out.reshape(N_CTX * TOK_DEV, D)
```

```python
import functools
import math

import jax
import jax.numpy as jnp
from jax import lax
from jax.experimental import pallas as pl
from jax.experimental.pallas import tpu as pltpu
from jax.sharding import PartitionSpec as P

HEAD_SIZE = 128
DISTANCES = (8, 4, 2, 1)
SLOT = {8: 4, 4: 3, 2: 2, 1: 1}
MESH = pl.DeviceIdType.MESH
FAR = 1e30


def block_kernel(
    n,
    with_residual,
    q_hbm,
    k_hbm,
    v_hbm,
    res_hbm,
    w_hbm,
    out_hbm,
    kv,
    q_vm,
    w_vm,
    res_vm,
    acc,
    out_vm,
    att,
    own_sem,
    q_sem,
    w_sem,
    res_sem,
    out_sem,
    send_sem,
    recv_sem,
):
    heads = q_vm.shape[0]
    rows = q_vm.shape[1]
    group = q_vm.shape[2] // HEAD_SIZE
    width = acc.shape[1]
    chunks = 2 * heads
    me = lax.axis_index("ctx")

    def own_copy(c):
        source = k_hbm if c % 2 == 0 else v_hbm
        return pltpu.make_async_copy(
            source.at[:, pl.ds((c // 2) * HEAD_SIZE, HEAD_SIZE)],
            kv.at[c, pl.ds(0, rows), :],
            own_sem.at[c],
        )

    def q_copy(h):
        return pltpu.make_async_copy(
            q_hbm.at[:, pl.ds(h * group * HEAD_SIZE, group * HEAD_SIZE)],
            q_vm.at[h],
            q_sem.at[h],
        )

    def w_copy(h):
        depth = group * HEAD_SIZE
        return pltpu.make_async_copy(
            w_hbm.at[pl.ds(h * depth, depth), :], w_vm.at[h], w_sem.at[h]
        )

    for c in range(chunks):
        own_copy(c).start()
    for h in range(heads):
        q_copy(h).start()
    if with_residual:
        res_copy = pltpu.make_async_copy(res_hbm, res_vm, res_sem)
        res_copy.start()
    for h in range(heads):
        w_copy(h).start()

    def bit(distance):
        return (me // distance) % 2

    def partner(distance):
        return me + distance * (1 - 2 * bit(distance))

    barrier = pltpu.get_barrier_semaphore()
    for distance in (4, 2, 1):
        pl.semaphore_signal(
            barrier, inc=1, device_id={"ctx": partner(distance)}, device_id_type=MESH
        )

    for peer in ((me + 8) % n, (me + n - 8) % n):
        pl.semaphore_signal(barrier, inc=1, device_id={"ctx": peer}, device_id_type=MESH)
    pl.semaphore_wait(barrier, 5)

    def send(c, distance, source, target):
        return pltpu.make_async_remote_copy(
            src_ref=kv.at[c, pl.ds(source * rows, rows), :],
            dst_ref=kv.at[c, pl.ds(SLOT[distance] * rows, rows), :],
            send_sem=send_sem.at[SLOT[distance] - 1, c],
            recv_sem=recv_sem.at[SLOT[distance] - 1, c],
            device_id={"ctx": target},
            device_id_type=MESH,
        )

    def sends_own(distance):
        return (me + 8 < n) if distance == 8 else (bit(distance) == 0)

    def sends_on(distance):
        return (bit(distance) == 1) & (me >= 2 * distance)

    for c in range(chunks):
        own_copy(c).wait()
        for distance in DISTANCES:
            @pl.when(sends_own(distance))
            def _():
                target = me + 8 if distance == 8 else partner(distance)
                send(c, distance, 0, target).start()

    for distance in DISTANCES:
        @pl.when(me < distance)
        def _():
            @pl.loop(0, chunks)
            def _(c):
                kv[c, pl.ds(SLOT[distance] * rows, rows), :] = jnp.zeros(
                    (rows, HEAD_SIZE), kv.dtype
                )

    if with_residual:
        res_copy.wait()
        acc[...] = res_vm[...].astype(jnp.float32)
    else:
        acc[...] = jnp.zeros_like(acc)

    def receive(c, distance):
        @pl.when(me >= distance)
        def _():
            send(c, distance, 0, me).wait_recv()

        if distance > 1:
            lower = distance // 2
            @pl.when(sends_on(lower))
            def _():
                send(c, lower, SLOT[distance], partner(lower)).start()

    def turn(t):
        for lag, distance in enumerate(DISTANCES):
            @pl.when((t >= lag) & (t < chunks + lag))
            def _():
                receive(t - lag, distance)

    unit = math.log2(math.e) / math.sqrt(HEAD_SIZE)
    away = {d: jnp.where(me >= d, 0.0, FAR) for d in DISTANCES}

    def attend(h, which):
        key = kv[2 * h]
        value = kv[2 * h + 1]
        value = jnp.concatenate([value, jnp.ones_like(value)], axis=1)
        row = lax.broadcasted_iota(jnp.int32, (rows, rows), 0)
        col = lax.broadcasted_iota(jnp.int32, (rows, rows), 1)
        all_scores = [
            lax.dot_general(
                q_vm[h, :, j * HEAD_SIZE : (j + 1) * HEAD_SIZE],
                key,
                (((1,), (1,)), ((), ())),
                preferred_element_type=jnp.float32,
            )
            for j in which
        ]
        for j, scores in zip(which, all_scores):
            own = jnp.where(col <= row, scores[:, :rows], -FAR)
            peak = jnp.max(own, axis=1, keepdims=True)
            parts = {0: own}
            for d in DISTANCES:
                at = SLOT[d]
                parts[at] = scores[:, at * rows : (at + 1) * rows]
                peak = jnp.maximum(
                    peak, jnp.max(parts[at], axis=1, keepdims=True) - away[d]
                )
            peak = peak * unit
            raised = [jnp.exp2(parts[0] * unit - peak).astype(jnp.bfloat16)]
            for d in reversed(DISTANCES):
                raised.append(
                    jnp.exp2(parts[SLOT[d]] * unit - (peak + away[d])).astype(jnp.bfloat16)
                )
            raised = jnp.concatenate(raised, axis=1)
            mixed = jnp.dot(raised, value, preferred_element_type=jnp.float32)
            mixed = mixed[:, :HEAD_SIZE] / mixed[:, HEAD_SIZE:]
            att[:, j * HEAD_SIZE : (j + 1) * HEAD_SIZE] = mixed.astype(jnp.bfloat16)

    lead = 2
    half = group // 2

    @pl.loop(0, heads + lead)
    def _(i):
        h = i - lead
        turn(2 * i)

        @pl.when(h >= 0)
        def _():
            q_copy(h).wait()
            attend(h, range(half))

        turn(2 * i + 1)

        @pl.when(h >= 0)
        def _():
            attend(h, range(half, group))
            w_copy(h).wait()
            step = min(1024, width)
            for at in range(0, width, step):
                acc[:, at : at + step] += jnp.dot(
                    att[...],
                    w_vm[h, :, at : at + step],
                    preferred_element_type=jnp.float32,
                )

    out_vm[...] = acc[...].astype(out_vm.dtype)
    out_copy = pltpu.make_async_copy(out_vm, out_hbm, out_sem)
    out_copy.start()

    for distance in DISTANCES:
        sent = sends_own(distance)
        if distance < 8:
            sent = sent | sends_on(distance)

        @pl.when(sent)
        def _():
            @pl.loop(0, chunks)
            def _(c):
                send(c, distance, 0, me).wait_send()

    out_copy.wait()


def on_device(n, hid, queries, keys, values, residual, out_weight):
    rows, columns = queries.shape
    heads = keys.shape[1] // HEAD_SIZE
    width = out_weight.shape[1]
    group_columns = columns // heads
    chunks = 2 * heads
    with_residual = hid == 1
    out_type = jnp.bfloat16 if with_residual else jnp.float32
    result = pl.pallas_call(
        functools.partial(block_kernel, n, with_residual),
        out_shape=jax.ShapeDtypeStruct((rows, width), out_type),
        in_specs=[pl.BlockSpec(memory_space=pl.ANY)] * 5,
        out_specs=pl.BlockSpec(memory_space=pl.ANY),
        scratch_shapes=[
            pltpu.VMEM((chunks, 5 * rows, HEAD_SIZE), jnp.bfloat16),
            pltpu.VMEM((heads, rows, group_columns), jnp.bfloat16),
            pltpu.VMEM((heads, group_columns, width), jnp.bfloat16),
            pltpu.VMEM(residual.shape, jnp.bfloat16),
            pltpu.VMEM((rows, width), jnp.float32),
            pltpu.VMEM((rows, width), out_type),
            pltpu.VMEM((rows, group_columns), jnp.bfloat16),
            pltpu.SemaphoreType.DMA((chunks,)),
            pltpu.SemaphoreType.DMA((heads,)),
            pltpu.SemaphoreType.DMA((heads,)),
            pltpu.SemaphoreType.DMA,
            pltpu.SemaphoreType.DMA,
            pltpu.SemaphoreType.DMA((4, chunks)),
            pltpu.SemaphoreType.DMA((4, chunks)),
        ],
        compiler_params=pltpu.CompilerParams(
            collective_id=0, has_side_effects=True, vmem_limit_bytes=60 * 1024 * 1024
        ),
    )(queries, keys, values, residual, out_weight)
    if with_residual:
        return result
    summed = lax.psum_scatter(result, "hid", scatter_dimension=1, tiled=True)
    return (residual.astype(jnp.float32) + summed).astype(jnp.bfloat16)


def solution(mesh):
    return jax.shard_map(
        functools.partial(on_device, mesh.shape["ctx"], mesh.shape["hid"]),
        mesh=mesh,
        in_specs=(
            P("ctx", "hid"),
            P("ctx", "hid"),
            P("ctx", "hid"),
            P("ctx", "hid"),
            P("hid", None),
        ),
        out_specs=P("ctx", "hid"),
        check_vma=False,
    )
```

```python
import functools
import math

import jax
import jax.numpy as jnp
from jax import lax
from jax.experimental import pallas as pl
from jax.experimental.pallas import tpu as pltpu
from jax.sharding import PartitionSpec as P

HEAD_SIZE = 128
DISTANCES = (8, 4, 2, 1)
SLOT = {8: 4, 4: 3, 2: 2, 1: 1}
MESH = pl.DeviceIdType.MESH
FAR = 1e30


def block_kernel(
    n,
    with_residual,
    q_hbm,
    k_hbm,
    v_hbm,
    res_hbm,
    w_hbm,
    out_ref,
    kv,
    q_vm,
    w_vm,
    res_vm,
    acc,
    att,
    own_sem,
    q_sem,
    w_sem,
    res_sem,
    send_sem,
    recv_sem,
):
    heads = q_vm.shape[0]
    rows = q_vm.shape[1]
    group = q_vm.shape[2] // HEAD_SIZE
    width = acc.shape[1]
    chunks = 2 * heads
    me = lax.axis_index("ctx")

    def own_copy(c):
        source = k_hbm if c % 2 == 0 else v_hbm
        return pltpu.make_async_copy(
            source.at[:, pl.ds((c // 2) * HEAD_SIZE, HEAD_SIZE)],
            kv.at[c, pl.ds(0, rows), :],
            own_sem.at[c],
        )

    def q_copy(h):
        return pltpu.make_async_copy(
            q_hbm.at[:, pl.ds(h * group * HEAD_SIZE, group * HEAD_SIZE)],
            q_vm.at[h],
            q_sem.at[h],
        )

    def w_copy(h):
        depth = group * HEAD_SIZE
        return pltpu.make_async_copy(
            w_hbm.at[pl.ds(h * depth, depth), :], w_vm.at[h], w_sem.at[h]
        )

    for c in range(chunks):
        own_copy(c).start()
    def bit(distance):
        return (me // distance) % 2

    def partner(distance):
        return me + distance * (1 - 2 * bit(distance))

    barrier = pltpu.get_barrier_semaphore()
    for distance in (4, 2, 1):
        pl.semaphore_signal(
            barrier, inc=1, device_id={"ctx": partner(distance)}, device_id_type=MESH
        )

    for peer in ((me + 8) % n, (me + n - 8) % n):
        pl.semaphore_signal(barrier, inc=1, device_id={"ctx": peer}, device_id_type=MESH)
    pl.semaphore_wait(barrier, 5)

    def send(c, distance, source, target):
        return pltpu.make_async_remote_copy(
            src_ref=kv.at[c, pl.ds(source * rows, rows), :],
            dst_ref=kv.at[c, pl.ds(SLOT[distance] * rows, rows), :],
            send_sem=send_sem.at[SLOT[distance] - 1, c],
            recv_sem=recv_sem.at[SLOT[distance] - 1, c],
            device_id={"ctx": target},
            device_id_type=MESH,
        )

    def sends_own(distance):
        return (me + 8 < n) if distance == 8 else (bit(distance) == 0)

    def sends_on(distance):
        return (bit(distance) == 1) & (me >= 2 * distance)

    for c in range(chunks):
        own_copy(c).wait()
        for distance in DISTANCES:
            @pl.when(sends_own(distance))
            def _():
                target = me + 8 if distance == 8 else partner(distance)
                send(c, distance, 0, target).start()

    if with_residual:
        res_copy = pltpu.make_async_copy(res_hbm, res_vm, res_sem)
        res_copy.start()
    for h in range(heads):
        q_copy(h).start()

    for distance in DISTANCES:
        @pl.when(me < distance)
        def _():
            @pl.loop(0, chunks)
            def _(c):
                kv[c, pl.ds(SLOT[distance] * rows, rows), :] = jnp.zeros(
                    (rows, HEAD_SIZE), kv.dtype
                )

    if with_residual:
        res_copy.wait()
        acc[...] = res_vm[...].astype(jnp.float32)
    else:
        acc[...] = jnp.zeros_like(acc)

    def receive(c, distance):
        @pl.when(me >= distance)
        def _():
            send(c, distance, 0, me).wait_recv()

        if distance > 1:
            lower = distance // 2
            @pl.when(sends_on(lower))
            def _():
                send(c, lower, SLOT[distance], partner(lower)).start()

    def turn(t):
        for lag, distance in enumerate(DISTANCES):
            @pl.when((t >= lag) & (t < chunks + lag))
            def _():
                receive(t - lag, distance)

    unit = math.log2(math.e) / math.sqrt(HEAD_SIZE)
    away = {d: jnp.where(me >= d, 0.0, FAR) for d in DISTANCES}

    def attend(h, which):
        key = kv[2 * h]
        value = kv[2 * h + 1]
        value = jnp.concatenate([value, jnp.ones_like(value)], axis=1)
        row = lax.broadcasted_iota(jnp.int32, (rows, rows), 0)
        col = lax.broadcasted_iota(jnp.int32, (rows, rows), 1)
        all_scores = [
            lax.dot_general(
                q_vm[h, :, j * HEAD_SIZE : (j + 1) * HEAD_SIZE],
                key,
                (((1,), (1,)), ((), ())),
                preferred_element_type=jnp.float32,
            )
            for j in which
        ]
        for j, scores in zip(which, all_scores):
            own = jnp.where(col <= row, scores[:, :rows], -FAR)
            peak = jnp.max(own, axis=1, keepdims=True)
            parts = {0: own}
            for d in DISTANCES:
                at = SLOT[d]
                parts[at] = scores[:, at * rows : (at + 1) * rows]
                peak = jnp.maximum(
                    peak, jnp.max(parts[at], axis=1, keepdims=True) - away[d]
                )
            peak = peak * unit
            raised = [jnp.exp2(parts[0] * unit - peak).astype(jnp.bfloat16)]
            for d in reversed(DISTANCES):
                raised.append(
                    jnp.exp2(parts[SLOT[d]] * unit - (peak + away[d])).astype(jnp.bfloat16)
                )
            raised = jnp.concatenate(raised, axis=1)
            mixed = jnp.dot(raised, value, preferred_element_type=jnp.float32)
            mixed = mixed[:, :HEAD_SIZE] / mixed[:, HEAD_SIZE:]
            att[:, j * HEAD_SIZE : (j + 1) * HEAD_SIZE] = mixed.astype(jnp.bfloat16)

    lead = 2
    half = group // 2

    @pl.loop(0, heads + lead)
    def _(i):
        h = i - lead
        turn(2 * i)

        @pl.when(i < heads)
        def _():
            w_copy(i).start()

        @pl.when(h >= 0)
        def _():
            q_copy(h).wait()
            attend(h, range(half))

        turn(2 * i + 1)

        @pl.when(h >= 0)
        def _():
            attend(h, range(half, group))
            w_copy(h).wait()
            step = min(1024, width)
            for at in range(0, width, step):
                acc[:, at : at + step] += jnp.dot(
                    att[...],
                    w_vm[h, :, at : at + step],
                    preferred_element_type=jnp.float32,
                )

    out_ref[...] = acc[...].astype(out_ref.dtype)

    for distance in DISTANCES:
        sent = sends_own(distance)
        if distance < 8:
            sent = sent | sends_on(distance)

        @pl.when(sent)
        def _():
            @pl.loop(0, chunks)
            def _(c):
                send(c, distance, 0, me).wait_send()


def on_device(n, hid, queries, keys, values, residual, out_weight):
    rows, columns = queries.shape
    heads = keys.shape[1] // HEAD_SIZE
    width = out_weight.shape[1]
    group_columns = columns // heads
    chunks = 2 * heads
    with_residual = hid == 1
    out_type = jnp.bfloat16 if with_residual else jnp.float32
    result = pl.pallas_call(
        functools.partial(block_kernel, n, with_residual),
        out_shape=pltpu.VMEM((rows, width), out_type),
        in_specs=[pl.BlockSpec(memory_space=pl.ANY)] * 5,
        out_specs=pl.BlockSpec(memory_space=pltpu.VMEM),
        scratch_shapes=[
            pltpu.VMEM((chunks, 5 * rows, HEAD_SIZE), jnp.bfloat16),
            pltpu.VMEM((heads, rows, group_columns), jnp.bfloat16),
            pltpu.VMEM((heads, group_columns, width), jnp.bfloat16),
            pltpu.VMEM(residual.shape, jnp.bfloat16),
            pltpu.VMEM((rows, width), jnp.float32),
            pltpu.VMEM((rows, group_columns), jnp.bfloat16),
            pltpu.SemaphoreType.DMA((chunks,)),
            pltpu.SemaphoreType.DMA((heads,)),
            pltpu.SemaphoreType.DMA((heads,)),
            pltpu.SemaphoreType.DMA,
            pltpu.SemaphoreType.DMA((4, chunks)),
            pltpu.SemaphoreType.DMA((4, chunks)),
        ],
        compiler_params=pltpu.CompilerParams(
            collective_id=0, has_side_effects=True, vmem_limit_bytes=54 * 1024 * 1024
        ),
    )(queries, keys, values, residual, out_weight)
    if with_residual:
        return result
    summed = lax.psum_scatter(result, "hid", scatter_dimension=1, tiled=True)
    return (residual.astype(jnp.float32) + summed).astype(jnp.bfloat16)


def solution(mesh):
    return jax.shard_map(
        functools.partial(on_device, mesh.shape["ctx"], mesh.shape["hid"]),
        mesh=mesh,
        in_specs=(
            P("ctx", "hid"),
            P("ctx", "hid"),
            P("ctx", "hid"),
            P("ctx", "hid"),
            P("hid", None),
        ),
        out_specs=P("ctx", "hid"),
        check_vma=False,
    )
```
